128 devices in a mesh: pipe: 8 (over y, z_lo), rep: 16 (over z_hi, x, core).
Axes of the slice: x: 4, y: 4, z: 4 (z_hi: 2, z_lo: 2; z = z_hi * 2 + z_lo), core: 2. Of those that a mesh axis runs over, the one named last changes fastest.
Arguments:
- activations: bfloat16 [8, 2, 2048, 14336], P('pipe', None, 'rep'), may hold values from -6 to 6
- upstream: bfloat16 [8, 2048, 14336], P('pipe', 'rep'), may hold values from -6 to 6
- final_grad: bfloat16 [2048, 14336], P('rep'), may hold values from -6 to 6
- w_in: bfloat16 [8, 64, 14336], P('pipe'), may hold values from -0.375 to 0.375
- w_out: bfloat16 [8, 64, 14336], P('pipe'), may hold values from -0.375 to 0.375
- momentum: bfloat16 [8, 2, 64, 14336], P('pipe'), may hold values from -80 to 80
- worker_error: bfloat16 [8, 16, 2, 64, 14336], P('pipe', 'rep'), may hold values from -8 to 8
- server_error: bfloat16 [8, 2, 64, 14336], P('pipe', None, None, 'rep'), may hold values from -8 to 8
Outputs:
- input_grads: bfloat16 [8, 2048, 14336], P('pipe', 'rep')
- new_momentum: bfloat16 [8, 2, 64, 14336], P('pipe')
- new_worker_error: bfloat16 [8, 16, 2, 64, 14336], P('pipe', 'rep')
- new_server_error: bfloat16 [8, 2, 64, 14336], P('pipe', None, None, 'rep')
The draws below stay inside these ranges and needn't reach their ends.
All inputs are finite; a program needn't handle non-finite values.
Results may differ from the reference program's by a relative error of at most 0.029.
Values may be sent and summed in bfloat16 or wider, within the bound.
A program may use at most 192 MiB of HBM per device.

```python
import jax
import jax.numpy as jnp
from jax import lax

D = 14336
K = 64
TOK_DEV = 128
GRP = 128
SECTIONS = 8
REPS = 16
BATCH_TOK = 2048
N_REP = 16


def draw_momentum(key, part):
    key = jax.random.fold_in(key, 7)
    row_key, column_key, entry_key = jax.random.split(key, 3)
    row_scale = 10.0 ** (jax.random.uniform(row_key, (SECTIONS, 2, K, 1), dtype=jnp.float32) - 0.5)
    column_scale = 10.0 ** (jax.random.uniform(column_key, (SECTIONS, 2, 1, D), dtype=jnp.float32) - 0.5)
    entries = jnp.clip(jax.random.normal(entry_key, (SECTIONS, 2, K, D), dtype=jnp.float32), -4.0, 4.0)
    return (2.0 * entries * row_scale * column_scale).astype(jnp.bfloat16)


def block_scale(own_key, shape, shards, smallest, high):
    level, own = 1.0, jax.random.fold_in(own_key, 6)
    for axis_at, shards_of in shards:
        draws = jnp.exp(jax.random.uniform(jax.random.fold_in(own, axis_at), (shards_of,), jnp.float32, smallest / len(shards), high / len(shards)))
        level = level * jnp.repeat(draws, shape[axis_at] // shards_of).reshape([-1 if axis == axis_at else 1 for axis in range(len(shape))])
    return level


def bell_draw(stream_key, shape, width, limit, cuts=(), kind=jnp.bfloat16):
    drawn = jax.random.normal(stream_key, shape, jnp.float32) * width
    if len(cuts) > 0:
        drawn = block_scale(stream_key, shape, cuts, -0.22, 0.18) * drawn
    return jnp.clip(drawn, min=-limit, max=limit).astype(kind)


def setup_inputs(seed: int = 0) -> dict:
    key_of = jax.random.split(jax.random.key(seed), 9)
    activations = bell_draw(key_of[0], (SECTIONS, 2, BATCH_TOK, D), 1.0, 6.0, ((0, 8), (2, 16)))
    upstream = bell_draw(key_of[1], (SECTIONS, BATCH_TOK, D), 1.0, 6.0, ((0, 8), (1, 16)))
    final_grad = bell_draw(key_of[2], (BATCH_TOK, D), 1.0, 6.0, ((0, 16),))
    w_in = bell_draw(key_of[3], (SECTIONS, K, D), (D // K) ** -0.5, 0.375, ((0, 8),))
    w_out = bell_draw(key_of[4], (SECTIONS, K, D), (D // K) ** -0.5, 0.375, ((0, 8),))
    momentum = draw_momentum(jax.random.fold_in(key_of[8], 71), 0)
    worker_error = bell_draw(key_of[6], (SECTIONS, REPS, 2, K, D), 2.0, 8.0, ((0, 8), (1, 16)))
    server_error = bell_draw(key_of[7], (SECTIONS, 2, K, D), 2.0, 8.0, ((0, 8), (3, 16)))
    return dict(activations=activations, upstream=upstream, final_grad=final_grad, w_in=w_in, w_out=w_out, momentum=momentum, worker_error=worker_error, server_error=server_error)


MOMENTUM_DECAY = 0.9
EPSILON = 1e-6
GELU_ROOT = 0.7978845608028654


def gelu_parts(hidden):
    argument = GELU_ROOT * (hidden + 0.044715 * hidden * hidden * hidden)
    tangent = jnp.tanh(argument)
    gelu_value = 0.5 * hidden * (1.0 + tangent)
    gelu_slope = 0.5 * (1.0 + tangent) + 0.5 * hidden * (1.0 - tangent * tangent) * GELU_ROOT * (1.0 + 3.0 * 0.044715 * hidden * hidden)
    return gelu_value, gelu_slope


def compress(values):
    layout = values.shape
    grouped = values.reshape(layout[:-1] + (layout[-1] // GRP, GRP))
    scales = (jnp.mean(jnp.abs(grouped), axis=-1) + EPSILON).astype(jnp.bfloat16)
    widened = scales.astype(jnp.float32)[..., None]
    levels = jnp.clip(grouped / widened, -1.0, 1.0).astype(jnp.bfloat16)
    leftover = grouped - widened * levels.astype(jnp.float32)
    return scales, levels.reshape(layout), leftover.reshape(layout)


def backward_part(features, weight_in, weight_out, incoming):
    hidden = jnp.dot(features, weight_in.T, preferred_element_type=jnp.float32)
    gelu_value, gelu_slope = gelu_parts(hidden)
    upward = jnp.dot(incoming, weight_out.T, preferred_element_type=jnp.float32)
    hidden_grad = (upward * gelu_slope).astype(jnp.bfloat16)
    passed = jnp.dot(hidden_grad, weight_in, preferred_element_type=jnp.float32).astype(jnp.bfloat16)
    return gelu_value.astype(jnp.bfloat16), hidden_grad, passed


def section_sync(features, hidden_grads, gelus, incoming, momentum, worker_error, server_error):
    replicas = N_REP

    def by_replica(stacked):
        return stacked.reshape((2, replicas, TOK_DEV) + stacked.shape[2:]).astype(jnp.float32)

    grad_in = jnp.einsum("mrtk,mrtd->rkd", by_replica(hidden_grads), by_replica(features))
    grad_out = jnp.einsum("mrtk,mrtd->rkd", by_replica(gelus), by_replica(incoming))
    gradient = jnp.stack([grad_in, grad_out], axis=1)
    blended = MOMENTUM_DECAY * momentum.astype(jnp.float32)[None] + (1.0 - MOMENTUM_DECAY) * gradient + worker_error.astype(jnp.float32)
    scales, levels, leftover = compress(blended)
    groups = D // GRP
    weighted = scales.astype(jnp.float32)[..., None] * levels.astype(jnp.float32).reshape(replicas, 2, K, groups, GRP)
    average = (jnp.sum(weighted, axis=0) / replicas).reshape(2, K, D)
    combined = average + server_error.astype(jnp.float32)
    server_scales, server_levels, server_left = compress(combined)
    restored = server_scales.astype(jnp.float32)[..., None] * server_levels.astype(jnp.float32).reshape(2, K, groups, GRP)
    return restored.reshape(2, K, D).astype(jnp.bfloat16), leftover.astype(jnp.bfloat16), server_left.astype(jnp.bfloat16)


def reference(activations, upstream, final_grad, w_in, w_out, momentum, worker_error, server_error):
    first_step = lax.map(lambda operands: backward_part(*operands), (activations[:, 0], w_in, w_out, upstream))
    incoming = jnp.concatenate([first_step[2][1:], final_grad[None]], axis=0)
    second_step = lax.map(lambda operands: backward_part(*operands), (activations[:, 1], w_in, w_out, incoming))
    gelus = jnp.stack([first_step[0], second_step[0]], axis=1)
    hidden_grads = jnp.stack([first_step[1], second_step[1]], axis=1)
    arriving = jnp.stack([upstream, incoming], axis=1)
    synced = lax.map(lambda operands: section_sync(*operands), (activations, hidden_grads, gelus, arriving, momentum, worker_error, server_error))
    return second_step[2], synced[0], synced[1], synced[2]
```

```python
import jax
import jax.numpy as jnp
from jax import lax
from jax.experimental import pallas as pl
from jax.experimental.pallas import tpu as pltpu
from jax.sharding import PartitionSpec as P

GRP = 128
D = 14336
K = 64
TOK = 128
BLK = 896
QTR = 3584
PIECE = 1792
GROUPS = BLK // GRP

MOMENTUM_DECAY = 0.9
EPSILON = 1e-06
GELU_ROOT = 0.7978845608028654

MESH = pl.DeviceIdType.MESH
OFFSETS = (2, 1, 3, 0)
F32 = jnp.float32
BF16 = jnp.bfloat16


def nt_dot(left, right):
    return lax.dot_general(left, right, (((1,), (1,)), ((), ())), preferred_element_type=F32)


def nn_dot(left, right):
    return lax.dot_general(left, right, (((1,), (0,)), ((), ())), preferred_element_type=F32)


def gelu_parts(hidden):
    argument = GELU_ROOT * (hidden + 0.044715 * hidden * hidden * hidden)
    tangent = jnp.tanh(argument)
    gelu_value = 0.5 * hidden * (1.0 + tangent)
    gelu_slope = 0.5 * (1.0 + tangent) + 0.5 * hidden * (1.0 - tangent * tangent) * GELU_ROOT * (
        1.0 + 3.0 * 0.044715 * hidden * hidden
    )
    return gelu_value, gelu_slope


def compress_group(values):
    mean = jnp.sum(jnp.abs(values), axis=1, keepdims=True) * (1.0 / GRP)
    scale = (mean + EPSILON).astype(BF16).astype(F32)
    level = jnp.clip(values * (1.0 / scale), -1.0, 1.0).astype(BF16).astype(F32)
    return scale * level


def kernel(
    acts, ups, fin, w_in, w_out, mom, err, serr,
    ig, nm, nw, ns,
    src, win_v, wout_v, wnx_v, mom_v, err_v, serr_v, nw_v, ig_v, nm_v, ns_v,
    v_sib, v_own, r_sib, x1, x2, z1, z2,
    slope_v, factor, hg_out, hg_next,
    l_a, l_w, l_u, l_o, l_misc, o_sem, nm_sem,
    wa_s, wa_r, wb_s, wb_r, wc_s, wc_r, hg_s, hg_r,
    sib_s, sib_r, x1_s, x1_r, x2_s, x2_r, z1_s, z1_r, z2_s, z2_r,
    gx_s, gx_r, gz_s, gz_r, gs_s, gs_r, hx_s, hx_r, hz_s, hz_r, ts_s, ts_r,
):
    p = lax.axis_index("pipe")
    r = lax.axis_index("rep")
    zh = r // 8
    x = lax.rem(r // 2, 4)
    c = lax.rem(r, 2)

    def at(zh_, x_, c_):
        return (p, zh_ * 8 + x_ * 2 + c_)

    def x_of(offset):
        return lax.rem(x + offset, 4)

    sibling = at(zh, x, 1 - c)
    partner = at(1 - zh, x, c)
    x_peer = [at(zh, x_of(o), c) for o in OFFSETS[:3]]
    prev = (lax.rem(p + 7, 8), r)
    nxt = (lax.rem(p + 1, 8), r)
    is_last = p == 7

    def cols(start, size):
        return pl.ds(pl.multiple_of(start, GRP), size)

    loads_a, loads_w, loads_u, loads_o = [], [], [], []
    for q in range(4):
        s = pl.ds(q * QTR, QTR)
        loads_a.append(pltpu.make_async_copy(acts.at[0, :, :, s], src.at[0, :, :, s], l_a.at[q]))
        loads_w.append(pltpu.make_async_copy(w_in.at[0, :, s], win_v.at[:, s], l_w.at[q]))
        loads_u.append(pltpu.make_async_copy(ups.at[0, :, s], src.at[1, 0, :, s], l_u.at[q]))
        loads_o.append(pltpu.make_async_copy(w_out.at[0, :, s], wout_v.at[:, s], l_o.at[q]))
    load_mom = pltpu.make_async_copy(mom.at[0], mom_v, l_misc.at[0])
    load_err = pltpu.make_async_copy(err.at[0, 0], err_v, l_misc.at[1])
    load_serr = pltpu.make_async_copy(serr.at[0], serr_v, l_misc.at[2])
    load_fin = pltpu.make_async_copy(fin, src.at[1, 1], l_misc.at[3])
    for q in range(4):
        loads_w[q].start()
        loads_a[q].start()
    for q in range(4):
        loads_o[q].start()
        loads_u[q].start()
    load_mom.start()
    load_err.start()
    load_serr.start()

    @pl.when(is_last)
    def _():
        load_fin.start()

    barrier = pltpu.get_barrier_semaphore()
    for device in [sibling, partner, nxt] + x_peer:
        pl.semaphore_signal(barrier, inc=1, device_id=device, device_id_type=MESH)
    pl.semaphore_wait(barrier, 6)

    sent = []

    def send(source, target, s_sem, r_sem, device):
        copy = pltpu.make_async_remote_copy(
            src_ref=source, dst_ref=target, send_sem=s_sem, recv_sem=r_sem, device_id=device, device_id_type=MESH
        )
        copy.start()
        sent.append(copy)
        return copy

    def piece(offset, core):
        return cols((x_of(offset) * 2 + core) * PIECE, PIECE)

    wa = [
        send(w_in.at[0, :, piece(o, c)], wnx_v.at[:, piece(o, c)], wa_s.at[i], wa_r.at[i], prev)
        for i, o in enumerate((0, 2))
    ]

    hidden = jnp.zeros((K, 2 * TOK), F32)
    for q in range(4):
        loads_w[q].wait()
        loads_a[q].wait()
        s = pl.ds(q * QTR, QTR)
        hidden = hidden + nt_dot(win_v[:, s], src[0, :, :, s].reshape(2 * TOK, QTR))
    gelu_value, gelu_slope = gelu_parts(hidden)
    factor[1] = gelu_value.astype(BF16)
    slope_v[...] = gelu_slope

    wc = []

    def to_sibling(i, offset):
        wc.append(send(wnx_v.at[:, piece(offset, c)], wnx_v.at[:, piece(offset, c)], wc_s.at[i], wc_r.at[i], sibling))

    wa[0].wait_recv()
    wb = [
        send(wnx_v.at[:, piece(0, c)], wnx_v.at[:, piece(0, c)], wb_s.at[i], wb_r.at[i], at(zh, x_of(o), c))
        for i, o in enumerate((1, 3))
    ]
    to_sibling(0, 0)

    up = jnp.zeros((K, TOK), F32)
    for q in range(4):
        loads_o[q].wait()
        loads_u[q].wait()
        s = pl.ds(q * QTR, QTR)
        up = up + nt_dot(wout_v[:, s], src[1, 0, :, s])
    hg = (up * slope_v[:, :TOK]).astype(BF16)
    factor[0, :, :TOK] = hg
    hg_out[...] = hg
    hg_copy = send(hg_out, hg_next, hg_s, hg_r, prev)

    wa[1].wait_recv()
    to_sibling(1, 2)
    wb[0].wait_recv()
    to_sibling(2, 3)
    wb[1].wait_recv()
    to_sibling(3, 1)
    for copy in wc:
        copy.wait_recv()
    hg_copy.wait_recv()

    @pl.when(jnp.logical_not(is_last))
    def _():
        left = hg_next[...].astype(F32).T.astype(BF16)

        def step(t, carry):
            s = cols(t * BLK, BLK)
            src[1, 1, :, s] = nn_dot(left, wnx_v[:, s]).astype(BF16)
            return carry

        lax.fori_loop(0, D // BLK, step, 0)

    @pl.when(is_last)
    def _():
        load_fin.wait()

    up = jnp.zeros((K, TOK), F32)
    for q in range(4):
        s = pl.ds(q * QTR, QTR)
        up = up + nt_dot(wout_v[:, s], src[1, 1, :, s])
    hg1 = up * slope_v[:, TOK:]
    factor[0, :, TOK:] = hg1.astype(BF16)

    load_mom.wait()
    load_err.wait()

    def half(k, core, target):
        x_to = x_of(OFFSETS[k])

        def step(i, carry):
            mat = i // 2
            zz = lax.rem(i, 2)
            base = (zz * 8 + x_to * 2 + core) * BLK
            block = cols(base, BLK)
            grad = nn_dot(factor[mat], src[mat, :, :, block].reshape(2 * TOK, BLK))
            for g in range(GROUPS):
                s = cols(base + g * GRP, GRP)
                blended = (
                    MOMENTUM_DECAY * mom_v[mat, :, s].astype(F32)
                    + (1.0 - MOMENTUM_DECAY) * grad[:, g * GRP : (g + 1) * GRP]
                    + err_v[mat, :, s].astype(F32)
                )
                value = compress_group(blended)
                nw_v[mat, :, s] = (blended - value).astype(BF16)
                target[k, mat, zz, :, g * GRP : (g + 1) * GRP] = value.astype(BF16)
            return carry

        lax.fori_loop(0, 4, step, 0)

    sib = []
    x1c, z1c = [], []

    def pair(k):
        sib[k].wait_recv()

        def step(i, carry):
            mat = i // 2
            zz = lax.rem(i, 2)
            v_own[k, mat, zz] = (v_own[k, mat, zz].astype(F32) + r_sib[k, mat, zz].astype(F32)).astype(BF16)
            return carry

        lax.fori_loop(0, 4, step, 0)
        z1c.append(send(v_own.at[k, 1, 1 - zh], z1.at[k], z1_s.at[k], z1_r.at[k], partner))
        if k < 3:
            x1c.append(send(v_own.at[k, 0], x1.at[k], x1_s.at[k], x1_r.at[k], x_peer[k]))

    for k in range(4):
        half(k, 1 - c, v_sib)
        sib.append(send(v_sib.at[k], r_sib.at[k], sib_s.at[k], sib_r.at[k], sibling))
        if k > 0:
            pair(k - 1)
        half(k, c, v_own)
    pair(3)
    store_nw = pltpu.make_async_copy(nw_v, nw.at[0, 0], o_sem.at[0])
    store_nw.start()

    z2c = []
    for k in range(3):
        z1c[k].wait_recv()
        v_own[k, 1, zh] = (v_own[k, 1, zh].astype(F32) + z1[k].astype(F32)).astype(BF16)
        z2c.append(send(v_own.at[k, 1, zh], z2.at[k], z2_s.at[k], z2_r.at[k], x_peer[k]))

    left = hg1.T.astype(BF16)

    def ig_step(t, carry):
        s = cols(t * BLK, BLK)
        ig_v[:, s] = nn_dot(left, win_v[:, s]).astype(BF16)
        return carry

    lax.fori_loop(0, D // BLK, ig_step, 0)
    store_ig = pltpu.make_async_copy(ig_v, ig.at[0], o_sem.at[1])
    store_ig.start()
    load_serr.wait()

    for k in range(3):
        x1c[k].wait_recv()
    other = 1 - zh
    v_own[3, 0, other] = (
        v_own[3, 0, other].astype(F32)
        + x1[0, other].astype(F32)
        + x1[1, other].astype(F32)
        + x1[2, other].astype(F32)
    ).astype(BF16)
    x2c = send(v_own.at[3, 0, other], x2, x2_s, x2_r, partner)

    my_cols = r * BLK

    def serve(mat, terms):
        for g in range(GROUPS):
            gs = slice(g * GRP, (g + 1) * GRP)
            total = v_own[3, mat, zh, :, gs].astype(F32)
            for term in terms:
                total = total + term[:, gs].astype(F32)
            combined = total * (1.0 / 16.0) + serr_v[mat, :, gs].astype(F32)
            value = compress_group(combined)
            ns_v[mat, :, gs] = (combined - value).astype(BF16)
            nm_v[mat, :, cols(my_cols + g * GRP, GRP)] = value.astype(BF16)

    z1c[3].wait_recv()
    for k in range(3):
        z2c[k].wait_recv()
    serve(1, [z1.at[3], z2.at[0], z2.at[1], z2.at[2]])
    x2c.wait_recv()
    serve(0, [x1.at[0, zh], x1.at[1, zh], x1.at[2, zh], x2])
    store_ns = pltpu.make_async_copy(ns_v, ns.at[0], o_sem.at[2])
    store_ns.start()

    def block_of(ref, zh_, x_, c_, mat=None):
        s = cols((zh_ * 8 + x_ * 2 + c_) * BLK, BLK)
        return ref.at[:, :, s] if mat is None else ref.at[mat, :, s]

    stored = []

    def store(zh_, x_, c_, mat=None):
        copy = pltpu.make_async_copy(
            block_of(nm_v, zh_, x_, c_, mat), block_of(nm.at[0], zh_, x_, c_, mat), nm_sem.at[len(stored)]
        )
        copy.start()
        stored.append(copy)

    def push(zh_, x_, mat, s_sem, r_sem, device):
        b = block_of(nm_v, zh_, x_, c, mat)
        return send(b, b, s_sem, r_sem, device)

    sibs = []

    def share(zh_, x_, mat):
        i = len(sibs)
        sibs.append((push(zh_, x_, mat, gs_s.at[i], gs_r.at[i], sibling), zh_, x_, mat))
        store(zh_, x_, c, mat)

    gx = [push(zh, x, None, gx_s.at[k], gx_r.at[k], x_peer[k]) for k in range(3)]
    gz = push(zh, x, None, gz_s, gz_r, partner)
    share(zh, x, None)
    gz.wait_recv()
    hx = [push(other, x, 0, hx_s.at[k], hx_r.at[k], x_peer[k]) for k in range(3)]
    share(other, x, None)
    hz = [None] * 3
    for k in (1, 2, 0):
        gx[k].wait_recv()
        x_from = x_of(4 - OFFSETS[k])
        hz[k] = push(zh, x_from, 1, hz_s.at[k], hz_r.at[k], partner)
        share(zh, x_from, None)
    for k in (1, 2, 0):
        x_from = x_of(4 - OFFSETS[k])
        hx[k].wait_recv()
        share(other, x_from, 0)
        hz[k].wait_recv()
        share(other, x_from, 1)
    for copy, zh_, x_, mat in sibs:
        copy.wait_recv()
        store(zh_, x_, 1 - c, mat)

    for copy in sent:
        copy.wait_send()
    for copy in stored:
        copy.wait()
    store_nw.wait()
    store_ig.wait()
    store_ns.wait()


def body(*arrays):
    dma = pltpu.SemaphoreType.DMA
    vmem = pltpu.VMEM
    return pl.pallas_call(
        kernel,
        name="cascade",
        out_shape=(
            jax.ShapeDtypeStruct((1, TOK, D), BF16),
            jax.ShapeDtypeStruct((1, 2, K, D), BF16),
            jax.ShapeDtypeStruct((1, 1, 2, K, D), BF16),
            jax.ShapeDtypeStruct((1, 2, K, BLK), BF16),
        ),
        in_specs=[pl.BlockSpec(memory_space=pl.ANY)] * 8,
        out_specs=(pl.BlockSpec(memory_space=pl.ANY),) * 4,
        scratch_shapes=[
            vmem((2, 2, TOK, D), BF16),
            vmem((K, D), BF16),
            vmem((K, D), BF16),
            vmem((K, D), BF16),
            vmem((2, K, D), BF16),
            vmem((2, K, D), BF16),
            vmem((2, K, BLK), BF16),
            vmem((2, K, D), BF16),
            vmem((TOK, D), BF16),
            vmem((2, K, D), BF16),
            vmem((2, K, BLK), BF16),
            vmem((4, 2, 2, K, BLK), BF16),
            vmem((4, 2, 2, K, BLK), BF16),
            vmem((4, 2, 2, K, BLK), BF16),
            vmem((3, 2, K, BLK), BF16),
            vmem((K, BLK), BF16),
            vmem((4, K, BLK), BF16),
            vmem((3, K, BLK), BF16),
            vmem((K, 2 * TOK), F32),
            vmem((2, K, 2 * TOK), BF16),
            vmem((K, TOK), BF16),
            vmem((K, TOK), BF16),
            dma((4,)), dma((4,)), dma((4,)), dma((4,)), dma((4,)), dma((3,)), dma((22,)),
            dma((2,)), dma((2,)), dma((2,)), dma((2,)), dma((4,)), dma((4,)), dma, dma,
            dma((4,)), dma((4,)), dma((3,)), dma((3,)), dma, dma, dma((4,)), dma((4,)), dma((3,)), dma((3,)),
            dma((3,)), dma((3,)), dma, dma, dma((11,)), dma((11,)), dma((3,)), dma((3,)), dma((3,)), dma((3,)),
            dma, dma,
        ],
        compiler_params=pltpu.CompilerParams(
            collective_id=0, has_side_effects=True, vmem_limit_bytes=56 * 2**20
        ),
        cost_estimate=pl.CostEstimate(flops=2_500_000_000, bytes_accessed=37_000_000, transcendentals=20_000),
    )(*arrays)


def solution(mesh):
    return jax.shard_map(
        body,
        mesh=mesh,
        in_specs=(
            P("pipe", None, "rep", None),
            P("pipe", "rep", None),
            P("rep", None),
            P("pipe", None, None),
            P("pipe", None, None),
            P("pipe", None, None, None),
            P("pipe", "rep", None, None, None),
            P("pipe", None, None, "rep"),
        ),
        out_specs=(
            P("pipe", "rep", None),
            P("pipe", None, None, None),
            P("pipe", "rep", None, None, None),
            P("pipe", None, None, "rep"),
        ),
        check_vma=False,
    )
```

```python
import jax
import jax.numpy as jnp
from jax import lax
from jax.experimental import pallas as pl
from jax.experimental.pallas import tpu as pltpu
from jax.sharding import PartitionSpec as P

GRP = 128
D = 14336
K = 64
TOK = 128
BLK = 896
QTR = 3584
PIECE = 1792
TWO = 2 * BLK
GROUPS = BLK // GRP

MOMENTUM_DECAY = 0.9
EPSILON = 1e-06
GELU_ROOT = 0.7978845608028654

MESH = pl.DeviceIdType.MESH
OFFSETS = (2, 1, 3, 0)
F32 = jnp.float32
BF16 = jnp.bfloat16


def nt_dot(left, right):
    return lax.dot_general(left, right, (((1,), (1,)), ((), ())), preferred_element_type=F32)


def nn_dot(left, right):
    return lax.dot_general(left, right, (((1,), (0,)), ((), ())), preferred_element_type=F32)


def gelu_parts(hidden):
    argument = GELU_ROOT * (hidden + 0.044715 * hidden * hidden * hidden)
    tangent = jnp.tanh(argument)
    gelu_value = 0.5 * hidden * (1.0 + tangent)
    gelu_slope = 0.5 * (1.0 + tangent) + 0.5 * hidden * (1.0 - tangent * tangent) * GELU_ROOT * (
        1.0 + 3.0 * 0.044715 * hidden * hidden
    )
    return gelu_value, gelu_slope


def compress_group(values):
    mean = jnp.sum(jnp.abs(values), axis=1, keepdims=True) * (1.0 / GRP)
    scale = (mean + EPSILON).astype(BF16).astype(F32)
    level = jnp.clip(values * (1.0 / scale), -1.0, 1.0).astype(BF16).astype(F32)
    return scale * level


def kernel(
    acts, ups, fin, w_in, w_out, mom, err, serr,
    ig_v, nm_v, nw_v, ns_v,
    src, win_v, wout_v, wnx_v, mom_v, err_v, serr_v,
    v_own, v_sum, r_sib, x1, x2, z1, z2,
    slope_v, factor, hg_out, hg_next, hg1_v, grad_a, grad_b,
    l_a, l_w, l_u, l_o, l_misc, s_sem, r_sem,
):
    p = lax.axis_index("pipe")
    r = lax.axis_index("rep")
    zh = r // 8
    x = lax.rem(r // 2, 4)
    c = lax.rem(r, 2)

    def at(zh_, x_, c_):
        return (p, zh_ * 8 + x_ * 2 + c_)

    def x_of(offset):
        return lax.rem(x + offset, 4)

    sibling = at(zh, x, 1 - c)
    partner = at(1 - zh, x, c)
    x_peer = [at(zh, x_of(o), c) for o in OFFSETS[:3]]
    prev = (lax.rem(p + 7, 8), r)
    nxt = (lax.rem(p + 1, 8), r)
    is_last = p == 7

    def cols(start, size):
        return pl.ds(pl.multiple_of(start, GRP), size)

    loads_a, loads_w, loads_u, loads_o = [], [], [], []
    for q in range(4):
        s = pl.ds(q * QTR, QTR)
        loads_a.append(pltpu.make_async_copy(acts.at[0, :, :, s], src.at[0, :, :, s], l_a.at[q]))
        loads_w.append(pltpu.make_async_copy(w_in.at[0, :, s], win_v.at[:, s], l_w.at[q]))
        loads_u.append(pltpu.make_async_copy(ups.at[0, :, s], src.at[1, 0, :, s], l_u.at[q]))
        loads_o.append(pltpu.make_async_copy(w_out.at[0, :, s], wout_v.at[:, s], l_o.at[q]))
    load_mom = pltpu.make_async_copy(mom.at[0], mom_v, l_misc.at[0])
    load_err = pltpu.make_async_copy(err.at[0, 0], err_v, l_misc.at[1])
    load_serr = pltpu.make_async_copy(serr.at[0], serr_v, l_misc.at[2])
    load_fin = pltpu.make_async_copy(fin, src.at[1, 1], l_misc.at[3])
    barrier = pltpu.get_barrier_semaphore()
    for device in [sibling, partner, nxt] + x_peer:
        pl.semaphore_signal(barrier, inc=1, device_id=device, device_id_type=MESH)
    for q in range(2):
        loads_w[q].start()
        loads_a[q].start()
    pl.semaphore_wait(barrier, 6)

    sent = []

    def send(source, target, device):
        copy = pltpu.make_async_remote_copy(
            src_ref=source,
            dst_ref=target,
            send_sem=s_sem.at[len(sent)],
            recv_sem=r_sem.at[len(sent)],
            device_id=device,
            device_id_type=MESH,
        )
        copy.start()
        sent.append(copy)
        return copy

    def finish():
        for copy in sent:
            copy.wait_send()

    def piece(offset, core):
        return cols((x_of(offset) * 2 + core) * PIECE, PIECE)

    wa = [send(w_in.at[0, :, piece(o, c)], wnx_v.at[:, piece(o, c)], prev) for o in (0, 2)]
    for q in range(2, 4):
        loads_w[q].start()
        loads_a[q].start()
    for q in range(4):
        loads_o[q].start()
        loads_u[q].start()

    @pl.when(is_last)
    def _():
        load_fin.start()

    hidden = jnp.zeros((K, 2 * TOK), F32)
    for q in range(4):
        loads_w[q].wait()
        loads_a[q].wait()
        s = pl.ds(q * QTR, QTR)
        hidden = hidden + nt_dot(win_v[:, s], src[0, :, :, s].reshape(2 * TOK, QTR))
    gelu_value, gelu_slope = gelu_parts(hidden)
    factor[1] = gelu_value.astype(BF16)
    slope_v[...] = gelu_slope

    wc = []

    def to_sibling(offset):
        wc.append(send(wnx_v.at[:, piece(offset, c)], wnx_v.at[:, piece(offset, c)], sibling))

    load_mom.start()
    load_err.start()
    load_serr.start()
    wa[0].wait_recv()
    wb = [send(wnx_v.at[:, piece(0, c)], wnx_v.at[:, piece(0, c)], at(zh, x_of(o), c)) for o in (1, 3)]
    to_sibling(0)

    up = jnp.zeros((K, TOK), F32)
    for q in range(4):
        loads_o[q].wait()
        loads_u[q].wait()
        s = pl.ds(q * QTR, QTR)
        up = up + nt_dot(wout_v[:, s], src[1, 0, :, s])
    hg = (up * slope_v[:, :TOK]).astype(BF16)
    factor[0, :, :TOK] = hg
    hg_out[...] = hg
    hg_copy = send(hg_out, hg_next, prev)

    wa[1].wait_recv()
    to_sibling(2)
    wb[0].wait_recv()
    to_sibling(3)
    wb[1].wait_recv()
    to_sibling(1)
    for copy in wc:
        copy.wait_recv()
    hg_copy.wait_recv()

    @pl.when(jnp.logical_not(is_last))
    def _():
        left = hg_next[...].astype(F32).T.astype(BF16)
        up = jnp.zeros((TOK, K), F32)
        for q in range(4):
            s = pl.ds(q * QTR, QTR)
            incoming = nn_dot(left, wnx_v[:, s]).astype(BF16)
            src[1, 1, :, s] = incoming
            up = up + nt_dot(incoming, wout_v[:, s])
        hg1_v[...] = up

    @pl.when(is_last)
    def _():
        load_fin.wait()
        up = jnp.zeros((TOK, K), F32)
        for q in range(4):
            s = pl.ds(q * QTR, QTR)
            up = up + nt_dot(src[1, 1, :, s], wout_v[:, s])
        hg1_v[...] = up

    hg1 = (hg1_v[...].T * slope_v[:, TOK:])
    factor[0, :, TOK:] = hg1.astype(BF16)

    load_mom.wait()
    load_err.wait()

    grads = (grad_a, grad_b)

    def base_of(k, zz):
        return (zz * 8 + x_of(OFFSETS[k]) * 2) * BLK

    def product(k, mat, zz):
        block = cols(base_of(k, zz), TWO)
        grads[zz][...] = nn_dot(factor[mat], src[mat, :, :, block].reshape(2 * TOK, TWO))

    def squeeze(k, mat, zz):
        base = base_of(k, zz)
        for g in range(2 * GROUPS):
            s = cols(base + g * GRP, GRP)
            blended = (
                MOMENTUM_DECAY * mom_v[mat, :, s].astype(F32)
                + (1.0 - MOMENTUM_DECAY) * grads[zz][:, g * GRP : (g + 1) * GRP]
                + err_v[mat, :, s].astype(F32)
            )
            value = compress_group(blended)
            nw_v[mat, :, s] = (blended - value).astype(BF16)
            at_g = g % GROUPS
            v_own[k, mat, g // GROUPS, zz, :, at_g * GRP : (at_g + 1) * GRP] = value.astype(BF16)

    sib = []
    x1c, z1c = [], []
    steps = [(k, mat) for k in range(4) for mat in range(2)]

    def pair(i):
        k, mat = steps[i]
        sib[i].wait_recv()
        for zz in range(2):
            v_sum[k, mat, zz] = (v_own[k, mat, c, zz].astype(F32) + r_sib[k, mat, zz].astype(F32)).astype(BF16)
        if mat == 1:
            z1c.append(send(v_sum.at[k, 1, 1 - zh], z1.at[k], partner))
        elif k < 3:
            x1c.append(send(v_sum.at[k, 0], x1.at[k], x_peer[k]))

    product(0, 0, 0)
    for i, (k, mat) in enumerate(steps):
        product(k, mat, 1)
        squeeze(k, mat, 0)
        if i < 7:
            product(*steps[i + 1], 0)
        squeeze(k, mat, 1)
        sib.append(send(v_own.at[k, mat, 1 - c], r_sib.at[k, mat], sibling))
        if i > 0:
            pair(i - 1)
    pair(7)

    z2c = []
    for k in range(3):
        z1c[k].wait_recv()
        v_sum[k, 1, zh] = (v_sum[k, 1, zh].astype(F32) + z1[k].astype(F32)).astype(BF16)
        z2c.append(send(v_sum.at[k, 1, zh], z2.at[k], x_peer[k]))

    left = hg1.T.astype(BF16)

    for q in range(2):
        s = pl.ds(q * (D // 2), D // 2)
        ig_v[:, s] = nn_dot(left, win_v[:, s]).astype(BF16)
    load_serr.wait()

    for k in range(3):
        x1c[k].wait_recv()
    other = 1 - zh
    v_sum[3, 0, other] = (
        v_sum[3, 0, other].astype(F32)
        + x1[0, other].astype(F32)
        + x1[1, other].astype(F32)
        + x1[2, other].astype(F32)
    ).astype(BF16)
    x2c = send(v_sum.at[3, 0, other], x2, partner)

    my_cols = r * BLK

    def serve(mat, terms):
        for g in range(GROUPS):
            gs = slice(g * GRP, (g + 1) * GRP)
            total = v_sum[3, mat, zh, :, gs].astype(F32)
            for term in terms:
                total = total + term[:, gs].astype(F32)
            combined = total * (1.0 / 16.0) + serr_v[mat, :, gs].astype(F32)
            value = compress_group(combined)
            ns_v[mat, :, gs] = (combined - value).astype(BF16)
            nm_v[mat, :, cols(my_cols + g * GRP, GRP)] = value.astype(BF16)

    z1c[3].wait_recv()
    for k in range(3):
        z2c[k].wait_recv()
    serve(1, [z1.at[3], z2.at[0], z2.at[1], z2.at[2]])
    x2c.wait_recv()
    serve(0, [x1.at[0, zh], x1.at[1, zh], x1.at[2, zh], x2])

    def push(zh_, x_, mat, device, rows=None):
        s = cols((zh_ * 8 + x_ * 2 + c) * BLK, BLK)
        block = nm_v.at[:, :, s] if mat is None else nm_v.at[mat, :, s] if rows is None else nm_v.at[mat, rows, s]
        return send(block, block, device)

    sibs = []

    def share(zh_, x_, mat, rows=None):
        sibs.append(push(zh_, x_, mat, sibling, rows))

    def x_from(offset):
        return x_of(4 - offset)

    x_next = {1: x_peer[1], 3: x_peer[2]}
    part = {1: pl.ds(0, K // 2), 3: pl.ds(K // 2, K // 2)}
    gx1 = {o: push(zh, x, 1, x_next[o]) for o in (1, 3)}
    gz0 = push(zh, x, 0, partner)
    gz1 = push(zh, x, 1, partner)
    gx0 = {o: push(zh, x, 0, x_next[o]) for o in (1, 3)}
    share(zh, x, None)
    gz0.wait_recv()
    hx = {o: push(other, x, 0, x_next[o]) for o in (1, 3)}
    share(other, x, 0)
    hz, far = {}, {}
    for o in (1, 3):
        gx1[o].wait_recv()
        far[1, o] = push(zh, x_from(o), 1, x_next[o], part[o])
        hz[o] = push(zh, x_from(o), 1, partner)
        share(zh, x_from(o), 1)
    gz1.wait_recv()
    share(other, x, 1)
    for o in (1, 3):
        gx0[o].wait_recv()
        far[0, o] = push(zh, x_from(o), 0, x_next[o], part[o])
        share(zh, x_from(o), 0)
    for o in (1, 3):
        far[1, o].wait_recv()
        hz[2, o] = push(zh, x_from(2), 1, partner, part[o])
        share(zh, x_from(2), 1, part[o])
    for o in (1, 3):
        hx[o].wait_recv()
        far[2, o] = push(other, x_from(o), 0, x_next[o], part[o])
        share(other, x_from(o), 0)
    for o in (1, 3):
        hz[o].wait_recv()
        share(other, x_from(o), 1)
        far[0, o].wait_recv()
        share(zh, x_from(2), 0, part[o])
    for o in (1, 3):
        hz[2, o].wait_recv()
        share(other, x_from(2), 1, part[o])
    for o in (1, 3):
        far[2, o].wait_recv()
        share(other, x_from(2), 0, part[o])
    for copy in sibs:
        copy.wait_recv()

    finish()


def store_kernel(a, b, c, d, a_out, b_out, c_out, d_out, sem):
    copies = [
        pltpu.make_async_copy(source, target, sem.at[i])
        for i, (source, target) in enumerate(((a, a_out), (b, b_out), (c, c_out), (d, d_out)))
    ]
    for copy in copies:
        copy.start()
    for copy in copies:
        copy.wait()


def body(*arrays):
    dma = pltpu.SemaphoreType.DMA
    vmem = pltpu.VMEM
    shapes = ((TOK, D), (2, K, D), (2, K, D), (2, K, BLK))
    results = pl.pallas_call(
        kernel,
        name="cascade",
        out_shape=tuple(pltpu.VMEM(shape, BF16) for shape in shapes),
        in_specs=[pl.BlockSpec(memory_space=pl.ANY)] * 8,
        out_specs=(pl.BlockSpec(memory_space=pltpu.VMEM),) * 4,
        scratch_shapes=[
            vmem((2, 2, TOK, D), BF16),
            vmem((K, D), BF16),
            vmem((K, D), BF16),
            vmem((K, D), BF16),
            vmem((2, K, D), BF16),
            vmem((2, K, D), BF16),
            vmem((2, K, BLK), BF16),
            vmem((4, 2, 2, 2, K, BLK), BF16),
            vmem((4, 2, 2, K, BLK), BF16),
            vmem((4, 2, 2, K, BLK), BF16),
            vmem((3, 2, K, BLK), BF16),
            vmem((K, BLK), BF16),
            vmem((4, K, BLK), BF16),
            vmem((3, K, BLK), BF16),
            vmem((K, 2 * TOK), F32),
            vmem((2, K, 2 * TOK), BF16),
            vmem((K, TOK), BF16),
            vmem((K, TOK), BF16),
            vmem((TOK, K), F32),
            vmem((K, TWO), F32),
            vmem((K, TWO), F32),
            dma((4,)), dma((4,)), dma((4,)), dma((4,)), dma((4,)), dma((80,)), dma((80,)),
        ],
        compiler_params=pltpu.CompilerParams(
            collective_id=0, has_side_effects=True, vmem_limit_bytes=44 * 2**20
        ),
        cost_estimate=pl.CostEstimate(flops=2_500_000_000, bytes_accessed=37_000_000, transcendentals=20_000),
    )(*arrays)
    stored = pl.pallas_call(
        store_kernel,
        name="store",
        out_shape=tuple(jax.ShapeDtypeStruct(shape, BF16) for shape in shapes),
        in_specs=[pl.BlockSpec(memory_space=pltpu.VMEM)] * 4,
        out_specs=(pl.BlockSpec(memory_space=pl.ANY),) * 4,
        scratch_shapes=[dma((4,))],
        compiler_params=pltpu.CompilerParams(vmem_limit_bytes=2 * 2**20),
        cost_estimate=pl.CostEstimate(flops=0, bytes_accessed=11_000_000, transcendentals=0),
    )(*results)
    return stored[0][None], stored[1][None], stored[2][None, None], stored[3][None]


def solution(mesh):
    return jax.shard_map(
        body,
        mesh=mesh,
        in_specs=(
            P("pipe", None, "rep", None),
            P("pipe", "rep", None),
            P("rep", None),
            P("pipe", None, None),
            P("pipe", None, None),
            P("pipe", None, None, None),
            P("pipe", "rep", None, None, None),
            P("pipe", None, None, "rep"),
        ),
        out_specs=(
            P("pipe", "rep", None),
            P("pipe", None, None, None),
            P("pipe", "rep", None, None, None),
            P("pipe", None, None, "rep"),
        ),
        check_vma=False,
    )
```

```python
import jax
import jax.numpy as jnp
from jax import lax
from jax.experimental import pallas as pl
from jax.experimental.pallas import tpu as pltpu
from jax.sharding import PartitionSpec as P

GRP = 128
D = 14336
K = 64
TOK = 128
BLK = 896
QTR = 3584
PIECE = 1792
TWO = 2 * BLK
GROUPS = BLK // GRP

MOMENTUM_DECAY = 0.9
EPSILON = 1e-06
GELU_ROOT = 0.7978845608028654

MESH = pl.DeviceIdType.MESH
OFFSETS = (2, 1, 3, 0)
F32 = jnp.float32
BF16 = jnp.bfloat16


def nt_dot(left, right):
    return lax.dot_general(left, right, (((1,), (1,)), ((), ())), preferred_element_type=F32)


def nn_dot(left, right):
    return lax.dot_general(left, right, (((1,), (0,)), ((), ())), preferred_element_type=F32)


def gelu_parts(hidden):
    argument = GELU_ROOT * (hidden + 0.044715 * hidden * hidden * hidden)
    tangent = jnp.tanh(argument)
    gelu_value = 0.5 * hidden * (1.0 + tangent)
    gelu_slope = 0.5 * (1.0 + tangent) + 0.5 * hidden * (1.0 - tangent * tangent) * GELU_ROOT * (
        1.0 + 3.0 * 0.044715 * hidden * hidden
    )
    return gelu_value, gelu_slope


def compress_group(values):
    mean = jnp.sum(jnp.abs(values), axis=1, keepdims=True) * (1.0 / GRP)
    scale = (mean + EPSILON).astype(BF16).astype(F32)
    level = jnp.clip(values * (1.0 / scale), -1.0, 1.0).astype(BF16).astype(F32)
    return scale * level


def kernel(
    acts, ups, fin, w_in, w_out, mom, err, serr,
    ig_v, nm_v, nw_v, ns_v,
    src, win_v, wout_v, wnx_v, mom_v, err_v, serr_v,
    v_own, v_sum, r_sib, x1, x2, z1, z2,
    slope_v, factor, hg_out, hg_next, hg1_v, grad_a, grad_b,
    l_a, l_w, l_u, l_o, l_misc, s_sem, r_sem,
):
    p = lax.axis_index("pipe")
    r = lax.axis_index("rep")
    zh = r // 8
    x = lax.rem(r // 2, 4)
    c = lax.rem(r, 2)

    def at(zh_, x_, c_):
        return (p, zh_ * 8 + x_ * 2 + c_)

    def x_of(offset):
        return lax.rem(x + offset, 4)

    sibling = at(zh, x, 1 - c)
    partner = at(1 - zh, x, c)
    x_peer = [at(zh, x_of(o), c) for o in OFFSETS[:3]]
    prev = (lax.rem(p + 7, 8), r)
    nxt = (lax.rem(p + 1, 8), r)
    is_last = p == 7

    def cols(start, size):
        return pl.ds(pl.multiple_of(start, GRP), size)

    loads_a, loads_w, loads_u, loads_o = [], [], [], []
    for q in range(4):
        s = pl.ds(q * QTR, QTR)
        loads_a.append(pltpu.make_async_copy(acts.at[0, :, :, s], src.at[0, :, :, s], l_a.at[q]))
        loads_w.append(pltpu.make_async_copy(w_in.at[0, :, s], win_v.at[:, s], l_w.at[q]))
        loads_u.append(pltpu.make_async_copy(ups.at[0, :, s], src.at[1, 0, :, s], l_u.at[q]))
        loads_o.append(pltpu.make_async_copy(w_out.at[0, :, s], wout_v.at[:, s], l_o.at[q]))
    load_mom = pltpu.make_async_copy(mom.at[0], mom_v, l_misc.at[0])
    load_err = pltpu.make_async_copy(err.at[0, 0], err_v, l_misc.at[1])
    load_serr = pltpu.make_async_copy(serr.at[0], serr_v, l_misc.at[2])
    load_fin = pltpu.make_async_copy(fin, src.at[1, 1], l_misc.at[3])
    barrier = pltpu.get_barrier_semaphore()
    for device in [sibling, partner, nxt] + x_peer:
        pl.semaphore_signal(barrier, inc=1, device_id=device, device_id_type=MESH)
    for q in range(2):
        loads_w[q].start()
        loads_a[q].start()
    pl.semaphore_wait(barrier, 6)

    sent = []

    def send(source, target, device):
        copy = pltpu.make_async_remote_copy(
            src_ref=source,
            dst_ref=target,
            send_sem=s_sem.at[len(sent)],
            recv_sem=r_sem.at[len(sent)],
            device_id=device,
            device_id_type=MESH,
        )
        copy.start()
        sent.append(copy)
        return copy

    def finish():
        for copy in sent:
            copy.wait_send()

    def piece(offset, core, part=None):
        start = (x_of(offset) * 2 + core) * PIECE
        return cols(start, PIECE) if part is None else cols(start + part * BLK, BLK)

    wa = [send(w_in.at[0, :, s], wnx_v.at[:, s], prev) for s in (piece(0, c, 0), piece(0, c, 1), piece(2, c))]
    for q in range(2, 4):
        loads_w[q].start()
        loads_a[q].start()
    for q in range(4):
        loads_o[q].start()
        loads_u[q].start()

    @pl.when(is_last)
    def _():
        load_fin.start()

    hidden = jnp.zeros((K, 2 * TOK), F32)
    for q in range(4):
        loads_w[q].wait()
        loads_a[q].wait()
        s = pl.ds(q * QTR, QTR)
        hidden = hidden + nt_dot(win_v[:, s], src[0, :, :, s].reshape(2 * TOK, QTR))
    gelu_value, gelu_slope = gelu_parts(hidden)
    factor[1] = gelu_value.astype(BF16)
    slope_v[...] = gelu_slope

    wc = []

    def to_sibling(s):
        wc.append(send(wnx_v.at[:, s], wnx_v.at[:, s], sibling))

    wb = {}

    def spread(i):
        wa[i].wait_recv()
        s = piece(0, c, i)
        for o in (1, 3):
            wb[i, o] = send(wnx_v.at[:, s], wnx_v.at[:, s], at(zh, x_of(o), c))
        to_sibling(s)

    load_mom.start()
    load_err.start()
    load_serr.start()
    spread(0)

    up = jnp.zeros((K, TOK), F32)
    for q in range(4):
        loads_o[q].wait()
        loads_u[q].wait()
        s = pl.ds(q * QTR, QTR)
        up = up + nt_dot(wout_v[:, s], src[1, 0, :, s])
    hg = (up * slope_v[:, :TOK]).astype(BF16)
    factor[0, :, :TOK] = hg
    hg_out[...] = hg
    hg_copy = send(hg_out, hg_next, prev)

    @pl.when(is_last)
    def _():
        load_fin.wait()
        up = jnp.zeros((TOK, K), F32)
        for q in range(4):
            s = pl.ds(q * QTR, QTR)
            up = up + nt_dot(src[1, 1, :, s], wout_v[:, s])
        hg1_v[...] = up

    @pl.when(jnp.logical_not(is_last))
    def _():
        hg1_v[...] = jnp.zeros_like(hg1_v)

    spread(1)
    for i in range(2):
        wb[i, 1].wait_recv()
        to_sibling(piece(3, c, i))
        wb[i, 3].wait_recv()
        to_sibling(piece(1, c, i))
    hg_copy.wait_recv()
    wa[2].wait_recv()
    to_sibling(piece(2, c))

    def passed_piece(offset, core):
        @pl.when(jnp.logical_not(is_last))
        def _():
            s = piece(offset, core)
            left = hg_next[...].astype(F32).T.astype(BF16)
            incoming = nn_dot(left, wnx_v[:, s]).astype(BF16)
            src[1, 1, :, s] = incoming
            hg1_v[...] += nt_dot(incoming, wout_v[:, s])

    for offset in (0, 3, 1, 2):
        passed_piece(offset, c)
    for offset, arrivals in ((0, (0, 1)), (3, (2, 4)), (1, (3, 5)), (2, (6,))):
        for i in arrivals:
            wc[i].wait_recv()
        passed_piece(offset, 1 - c)

    hg1 = hg1_v[...].T * slope_v[:, TOK:]
    factor[0, :, TOK:] = hg1.astype(BF16)

    load_mom.wait()
    load_err.wait()

    grads = (grad_a, grad_b)

    def base_of(k, zz):
        return (zz * 8 + x_of(OFFSETS[k]) * 2) * BLK

    def product(k, mat, zz):
        block = cols(base_of(k, zz), TWO)
        grads[zz][...] = nn_dot(factor[mat], src[mat, :, :, block].reshape(2 * TOK, TWO))

    def squeeze(k, mat, zz):
        base = base_of(k, zz)
        for g in range(2 * GROUPS):
            s = cols(base + g * GRP, GRP)
            blended = (
                MOMENTUM_DECAY * mom_v[mat, :, s].astype(F32)
                + (1.0 - MOMENTUM_DECAY) * grads[zz][:, g * GRP : (g + 1) * GRP]
                + err_v[mat, :, s].astype(F32)
            )
            value = compress_group(blended)
            nw_v[mat, :, s] = (blended - value).astype(BF16)
            at_g = g % GROUPS
            v_own[k, mat, g // GROUPS, zz, :, at_g * GRP : (at_g + 1) * GRP] = value.astype(BF16)

    sib = []
    x1c, z1c = [], []
    steps = [(k, mat) for k in range(4) for mat in range(2)]

    other = 1 - zh

    def pair(i):
        k, mat = steps[i]
        sib[i].wait_recv()
        for zz in range(2):
            v_sum[k, mat, zz] = (v_own[k, mat, c, zz].astype(F32) + r_sib[k, mat, zz].astype(F32)).astype(BF16)
        if mat == 1:
            z1c.append(send(v_sum.at[k, 1, other], z1.at[k], partner))
        elif k < 3:
            x1c.append(send(v_sum.at[k, 0, other], x1.at[k, 0], x_peer[k]))

    product(0, 0, 0)
    for i, (k, mat) in enumerate(steps):
        product(k, mat, 1)
        squeeze(k, mat, 0)
        if i < 7:
            product(*steps[i + 1], 0)
        squeeze(k, mat, 1)
        sib.append(send(v_own.at[k, mat, 1 - c], r_sib.at[k, mat], sibling))
        if i > 0:
            pair(i - 1)
        if i == 6:
            x1o = [send(v_sum.at[k, 0, zh], x1.at[k, 1], x_peer[k]) for k in range(3)]
    pair(7)

    z2c = []

    def second(k):
        z1c[k].wait_recv()
        v_sum[k, 1, zh] = (v_sum[k, 1, zh].astype(F32) + z1[k].astype(F32)).astype(BF16)
        z2c.append(send(v_sum.at[k, 1, zh], z2.at[k], x_peer[k]))

    second(0)
    left = hg1.T.astype(BF16)
    for q in range(2):
        s = pl.ds(q * (D // 2), D // 2)
        ig_v[:, s] = nn_dot(left, win_v[:, s]).astype(BF16)
    second(1)
    total = v_sum[3, 0, other].astype(F32)
    for k in range(3):
        x1c[k].wait_recv()
        total = total + x1[k, 0].astype(F32)
    v_sum[3, 0, other] = total.astype(BF16)
    x2c = send(v_sum.at[3, 0, other], x2, partner)
    second(2)
    load_serr.wait()
    my_cols = r * BLK

    def serve(mat, terms):
        for g in range(GROUPS):
            gs = slice(g * GRP, (g + 1) * GRP)
            total = v_sum[3, mat, zh, :, gs].astype(F32)
            for term in terms:
                total = total + term[:, gs].astype(F32)
            combined = total * (1.0 / 16.0) + serr_v[mat, :, gs].astype(F32)
            value = compress_group(combined)
            ns_v[mat, :, gs] = (combined - value).astype(BF16)
            nm_v[mat, :, cols(my_cols + g * GRP, GRP)] = value.astype(BF16)

    def push(zh_, x_, mat, device, rows=None):
        s = cols((zh_ * 8 + x_ * 2 + c) * BLK, BLK)
        block = nm_v.at[:, :, s] if mat is None else nm_v.at[mat, :, s] if rows is None else nm_v.at[mat, rows, s]
        return send(block, block, device)

    sibs = []

    def share(zh_, x_, mat, rows=None):
        sibs.append(push(zh_, x_, mat, sibling, rows))

    def x_from(offset):
        return x_of(4 - offset)

    x_next = {1: x_peer[1], 3: x_peer[2]}
    part = {1: pl.ds(0, K // 2), 3: pl.ds(K // 2, K // 2)}
    z1c[3].wait_recv()
    for k in range(3):
        z2c[k].wait_recv()
    serve(1, [z1.at[3], z2.at[0], z2.at[1], z2.at[2]])
    gx1 = {o: push(zh, x, 1, x_next[o]) for o in (1, 3)}
    gz1 = push(zh, x, 1, partner)
    share(zh, x, 1)
    for copy in x1o:
        copy.wait_recv()
    x2c.wait_recv()
    serve(0, [x1.at[0, 1], x1.at[1, 1], x1.at[2, 1], x2])
    gz0 = push(zh, x, 0, partner)
    gx0 = {o: push(zh, x, 0, x_next[o]) for o in (1, 3)}
    share(zh, x, 0)
    hz, far = {}, {}
    for o in (1, 3):
        gx1[o].wait_recv()
        far[1, o] = push(zh, x_from(o), 1, x_next[o], part[o])
        hz[o] = push(zh, x_from(o), 1, partner)
        share(zh, x_from(o), 1)
    gz0.wait_recv()
    hx = {o: push(other, x, 0, x_next[o]) for o in (1, 3)}
    share(other, x, 0)
    gz1.wait_recv()
    share(other, x, 1)
    for o in (1, 3):
        gx0[o].wait_recv()
        far[0, o] = push(zh, x_from(o), 0, x_next[o], part[o])
        share(zh, x_from(o), 0)
    for o in (1, 3):
        far[1, o].wait_recv()
        hz[2, o] = push(zh, x_from(2), 1, partner, part[o])
        share(zh, x_from(2), 1, part[o])
    for o in (1, 3):
        hx[o].wait_recv()
        far[2, o] = push(other, x_from(o), 0, x_next[o], part[o])
        share(other, x_from(o), 0)
    for o in (1, 3):
        hz[o].wait_recv()
        share(other, x_from(o), 1)
        far[0, o].wait_recv()
        share(zh, x_from(2), 0, part[o])
    for o in (1, 3):
        hz[2, o].wait_recv()
        share(other, x_from(2), 1, part[o])
    for o in (1, 3):
        far[2, o].wait_recv()
        share(other, x_from(2), 0, part[o])
    for copy in sibs:
        copy.wait_recv()

    finish()


def store_kernel(a, b, c, d, a_out, b_out, c_out, d_out, sem):
    copies = [
        pltpu.make_async_copy(source, target, sem.at[i])
        for i, (source, target) in enumerate(((a, a_out), (b, b_out), (c, c_out), (d, d_out)))
    ]
    for copy in copies:
        copy.start()
    for copy in copies:
        copy.wait()


def body(*arrays):
    dma = pltpu.SemaphoreType.DMA
    vmem = pltpu.VMEM
    shapes = ((TOK, D), (2, K, D), (2, K, D), (2, K, BLK))
    results = pl.pallas_call(
        kernel,
        name="cascade",
        out_shape=tuple(pltpu.VMEM(shape, BF16) for shape in shapes),
        in_specs=[pl.BlockSpec(memory_space=pl.ANY)] * 8,
        out_specs=(pl.BlockSpec(memory_space=pltpu.VMEM),) * 4,
        scratch_shapes=[
            vmem((2, 2, TOK, D), BF16),
            vmem((K, D), BF16),
            vmem((K, D), BF16),
            vmem((K, D), BF16),
            vmem((2, K, D), BF16),
            vmem((2, K, D), BF16),
            vmem((2, K, BLK), BF16),
            vmem((4, 2, 2, 2, K, BLK), BF16),
            vmem((4, 2, 2, K, BLK), BF16),
            vmem((4, 2, 2, K, BLK), BF16),
            vmem((3, 2, K, BLK), BF16),
            vmem((K, BLK), BF16),
            vmem((4, K, BLK), BF16),
            vmem((3, K, BLK), BF16),
            vmem((K, 2 * TOK), F32),
            vmem((2, K, 2 * TOK), BF16),
            vmem((K, TOK), BF16),
            vmem((K, TOK), BF16),
            vmem((TOK, K), F32),
            vmem((K, TWO), F32),
            vmem((K, TWO), F32),
            dma((4,)), dma((4,)), dma((4,)), dma((4,)), dma((4,)), dma((80,)), dma((80,)),
        ],
        compiler_params=pltpu.CompilerParams(
            collective_id=0, has_side_effects=True, vmem_limit_bytes=44 * 2**20
        ),
        cost_estimate=pl.CostEstimate(flops=2_500_000_000, bytes_accessed=37_000_000, transcendentals=20_000),
    )(*arrays)
    stored = pl.pallas_call(
        store_kernel,
        name="store",
        out_shape=tuple(jax.ShapeDtypeStruct(shape, BF16) for shape in shapes),
        in_specs=[pl.BlockSpec(memory_space=pltpu.VMEM)] * 4,
        out_specs=(pl.BlockSpec(memory_space=pl.ANY),) * 4,
        scratch_shapes=[dma((4,))],
        compiler_params=pltpu.CompilerParams(vmem_limit_bytes=2 * 2**20),
        cost_estimate=pl.CostEstimate(flops=0, bytes_accessed=11_000_000, transcendentals=0),
    )(*results)
    return stored[0][None], stored[1][None], stored[2][None, None], stored[3][None]


def solution(mesh):
    return jax.shard_map(
        body,
        mesh=mesh,
        in_specs=(
            P("pipe", None, "rep", None),
            P("pipe", "rep", None),
            P("rep", None),
            P("pipe", None, None),
            P("pipe", None, None),
            P("pipe", None, None, None),
            P("pipe", "rep", None, None, None),
            P("pipe", None, None, "rep"),
        ),
        out_specs=(
            P("pipe", "rep", None),
            P("pipe", None, None, None),
            P("pipe", "rep", None, None, None),
            P("pipe", None, None, "rep"),
        ),
        check_vma=False,
    )
```

```python
import jax
import jax.numpy as jnp
from jax import lax
from jax.experimental import pallas as pl
from jax.experimental.pallas import tpu as pltpu
from jax.sharding import PartitionSpec as P

GRP = 128
D = 14336
K = 64
TOK = 128
BLK = 896
QTR = 3584
PIECE = 1792
TWO = 2 * BLK
GROUPS = BLK // GRP

MOMENTUM_DECAY = 0.9
EPSILON = 1e-06
GELU_ROOT = 0.7978845608028654

MESH = pl.DeviceIdType.MESH
OFFSETS = (2, 1, 3, 0)
F32 = jnp.float32
BF16 = jnp.bfloat16


def nt_dot(left, right):
    return lax.dot_general(left, right, (((1,), (1,)), ((), ())), preferred_element_type=F32)


def nn_dot(left, right):
    return lax.dot_general(left, right, (((1,), (0,)), ((), ())), preferred_element_type=F32)


def gelu_parts(hidden):
    argument = GELU_ROOT * (hidden + 0.044715 * hidden * hidden * hidden)
    tangent = jnp.tanh(argument)
    gelu_value = 0.5 * hidden * (1.0 + tangent)
    gelu_slope = 0.5 * (1.0 + tangent) + 0.5 * hidden * (1.0 - tangent * tangent) * GELU_ROOT * (
        1.0 + 3.0 * 0.044715 * hidden * hidden
    )
    return gelu_value, gelu_slope


def compress_group(values):
    mean = jnp.sum(jnp.abs(values), axis=1, keepdims=True) * (1.0 / GRP)
    scale = (mean + EPSILON).astype(BF16).astype(F32)
    level = jnp.clip(values * (1.0 / scale), -1.0, 1.0).astype(BF16).astype(F32)
    return scale * level


def kernel(
    acts, ups, fin, w_in, w_out, mom, err, serr,
    ig_v, nm_v, nw_v, ns_v,
    src, win_v, wout_v, wnx_v, mom_v, err_v, serr_v,
    v_own, v_sum, r_sib, x1, x2, z1, z2,
    slope_v, factor, hg_out, hg_next, hg1_v, grad_a, grad_b,
    l_a, l_w, l_u, l_o, l_misc, s_sem, r_sem,
):
    p = lax.axis_index("pipe")
    r = lax.axis_index("rep")
    zh = r // 8
    x = lax.rem(r // 2, 4)
    c = lax.rem(r, 2)

    def at(zh_, x_, c_):
        return (p, zh_ * 8 + x_ * 2 + c_)

    def x_of(offset):
        return lax.rem(x + offset, 4)

    sibling = at(zh, x, 1 - c)
    partner = at(1 - zh, x, c)
    x_peer = [at(zh, x_of(o), c) for o in OFFSETS[:3]]
    prev = (lax.rem(p + 7, 8), r)
    nxt = (lax.rem(p + 1, 8), r)
    is_last = p == 7

    def cols(start, size):
        return pl.ds(pl.multiple_of(start, GRP), size)

    loads_a, loads_w, loads_u, loads_o = [], [], [], []
    for q in range(4):
        s = pl.ds(q * QTR, QTR)
        loads_a.append(pltpu.make_async_copy(acts.at[0, :, :, s], src.at[0, :, :, s], l_a.at[q]))
        loads_w.append(pltpu.make_async_copy(w_in.at[0, :, s], win_v.at[:, s], l_w.at[q]))
        loads_u.append(pltpu.make_async_copy(ups.at[0, :, s], src.at[1, 0, :, s], l_u.at[q]))
        loads_o.append(pltpu.make_async_copy(w_out.at[0, :, s], wout_v.at[:, s], l_o.at[q]))
    load_mom = pltpu.make_async_copy(mom.at[0], mom_v, l_misc.at[0])
    load_err = pltpu.make_async_copy(err.at[0, 0], err_v, l_misc.at[1])
    load_serr = pltpu.make_async_copy(serr.at[0], serr_v, l_misc.at[2])
    load_fin = pltpu.make_async_copy(fin, src.at[1, 1], l_misc.at[3])
    barrier = pltpu.get_barrier_semaphore()
    for device in [sibling, partner, nxt] + x_peer:
        pl.semaphore_signal(barrier, inc=1, device_id=device, device_id_type=MESH)
    for q in range(2):
        loads_w[q].start()
        loads_a[q].start()
    pl.semaphore_wait(barrier, 6)

    sent = []

    def send(source, target, device):
        copy = pltpu.make_async_remote_copy(
            src_ref=source,
            dst_ref=target,
            send_sem=s_sem.at[len(sent)],
            recv_sem=r_sem.at[len(sent)],
            device_id=device,
            device_id_type=MESH,
        )
        copy.start()
        sent.append(copy)
        return copy

    def finish():
        for copy in sent:
            copy.wait_send()

    def piece(offset, core, part=None):
        start = (x_of(offset) * 2 + core) * PIECE
        return cols(start, PIECE) if part is None else cols(start + part * BLK, BLK)

    wa = [send(w_in.at[0, :, s], wnx_v.at[:, s], prev) for s in (piece(0, c, 0), piece(0, c, 1), piece(2, c))]
    for q in range(2, 4):
        loads_w[q].start()
        loads_a[q].start()
    for q in range(4):
        loads_o[q].start()
        loads_u[q].start()

    @pl.when(is_last)
    def _():
        load_fin.start()

    hidden = jnp.zeros((K, 2 * TOK), F32)
    for q in range(4):
        loads_w[q].wait()
        loads_a[q].wait()
        s = pl.ds(q * QTR, QTR)
        hidden = hidden + nt_dot(win_v[:, s], src[0, :, :, s].reshape(2 * TOK, QTR))
    gelu_value, gelu_slope = gelu_parts(hidden)
    factor[1] = gelu_value.astype(BF16)
    slope_v[...] = gelu_slope

    wc = []

    def to_sibling(s):
        wc.append(send(wnx_v.at[:, s], wnx_v.at[:, s], sibling))

    wb = {}

    def spread(i):
        wa[i].wait_recv()
        s = piece(0, c, i)
        for o in (1, 3):
            wb[i, o] = send(wnx_v.at[:, s], wnx_v.at[:, s], at(zh, x_of(o), c))
        to_sibling(s)

    load_mom.start()
    load_err.start()
    load_serr.start()
    spread(0)

    up = jnp.zeros((K, TOK), F32)
    for q in range(4):
        loads_o[q].wait()
        loads_u[q].wait()
        s = pl.ds(q * QTR, QTR)
        up = up + nt_dot(wout_v[:, s], src[1, 0, :, s])
    hg = (up * slope_v[:, :TOK]).astype(BF16)
    factor[0, :, :TOK] = hg
    hg_out[...] = hg
    hg_copy = send(hg_out, hg_next, prev)

    @pl.when(is_last)
    def _():
        load_fin.wait()
        up = jnp.zeros((TOK, K), F32)
        for q in range(4):
            s = pl.ds(q * QTR, QTR)
            up = up + nt_dot(src[1, 1, :, s], wout_v[:, s])
        hg1_v[...] = up

    @pl.when(jnp.logical_not(is_last))
    def _():
        hg1_v[...] = jnp.zeros_like(hg1_v)

    spread(1)
    for i in range(2):
        wb[i, 1].wait_recv()
        to_sibling(piece(3, c, i))
        wb[i, 3].wait_recv()
        to_sibling(piece(1, c, i))
    hg_copy.wait_recv()
    wa[2].wait_recv()
    to_sibling(piece(2, c))

    def passed_piece(offset, core):
        @pl.when(jnp.logical_not(is_last))
        def _():
            s = piece(offset, core)
            left = hg_next[...].astype(F32).T.astype(BF16)
            incoming = nn_dot(left, wnx_v[:, s]).astype(BF16)
            src[1, 1, :, s] = incoming
            hg1_v[...] += nt_dot(incoming, wout_v[:, s])

    for offset in (0, 3, 1, 2):
        passed_piece(offset, c)
    for offset, arrivals in ((0, (0, 1)), (3, (2, 4)), (1, (3, 5)), (2, (6,))):
        for i in arrivals:
            wc[i].wait_recv()
        passed_piece(offset, 1 - c)

    hg1 = hg1_v[...].T * slope_v[:, TOK:]
    factor[0, :, TOK:] = hg1.astype(BF16)

    load_mom.wait()
    load_err.wait()

    grads = (grad_a, grad_b)

    def base_of(k, zz):
        return (zz * 8 + x_of(OFFSETS[k]) * 2) * BLK

    def product(k, mat, zz):
        block = cols(base_of(k, zz), TWO)
        grads[zz][...] = nn_dot(factor[mat], src[mat, :, :, block].reshape(2 * TOK, TWO))

    def squeeze(k, mat, zz):
        base = base_of(k, zz)
        for g in range(2 * GROUPS):
            s = cols(base + g * GRP, GRP)
            blended = (
                MOMENTUM_DECAY * mom_v[mat, :, s].astype(F32)
                + (1.0 - MOMENTUM_DECAY) * grads[zz][:, g * GRP : (g + 1) * GRP]
                + err_v[mat, :, s].astype(F32)
            )
            value = compress_group(blended)
            nw_v[mat, :, s] = (blended - value).astype(BF16)
            at_g = g % GROUPS
            v_own[k, mat, g // GROUPS, zz, :, at_g * GRP : (at_g + 1) * GRP] = value.astype(BF16)

    sib = []
    x1c, z1c = [], []
    steps = [(k, mat) for k in range(4) for mat in range(2)]

    other = 1 - zh

    def pair(i):
        k, mat = steps[i]
        sib[i].wait_recv()
        for zz in range(2):
            v_sum[k, mat, zz] = (v_own[k, mat, c, zz].astype(F32) + r_sib[k, mat, zz].astype(F32)).astype(BF16)
        if mat == 1:
            z1c.append(send(v_sum.at[k, 1, other], z1.at[k], partner))
        elif k < 3:
            x1c.append(send(v_sum.at[k, 0, other], x1.at[k, 0], x_peer[k]))

    product(0, 0, 0)
    for i, (k, mat) in enumerate(steps):
        product(k, mat, 1)
        squeeze(k, mat, 0)
        if i < 7:
            product(*steps[i + 1], 0)
        squeeze(k, mat, 1)
        sib.append(send(v_own.at[k, mat, 1 - c], r_sib.at[k, mat], sibling))
        if i > 0:
            pair(i - 1)
        if i == 5:
            x1o = [send(v_sum.at[k, 0, zh], x1.at[k, 1], x_peer[k]) for k in range(3)]
    pair(7)

    z2c = []

    def second(k):
        z1c[k].wait_recv()
        v_sum[k, 1, zh] = (v_sum[k, 1, zh].astype(F32) + z1[k].astype(F32)).astype(BF16)
        z2c.append(send(v_sum.at[k, 1, zh], z2.at[k], x_peer[k]))

    second(0)
    left = hg1.T.astype(BF16)
    for q in range(2):
        s = pl.ds(q * (D // 2), D // 2)
        ig_v[:, s] = nn_dot(left, win_v[:, s]).astype(BF16)
    second(1)
    total = v_sum[3, 0, other].astype(F32)
    for k in range(3):
        x1c[k].wait_recv()
        total = total + x1[k, 0].astype(F32)
    v_sum[3, 0, other] = total.astype(BF16)
    x2c = send(v_sum.at[3, 0, other], x2, partner)
    second(2)
    load_serr.wait()
    my_cols = r * BLK

    def serve(mat, terms):
        for g in range(GROUPS):
            gs = slice(g * GRP, (g + 1) * GRP)
            total = v_sum[3, mat, zh, :, gs].astype(F32)
            for term in terms:
                total = total + term[:, gs].astype(F32)
            combined = total * (1.0 / 16.0) + serr_v[mat, :, gs].astype(F32)
            value = compress_group(combined)
            ns_v[mat, :, gs] = (combined - value).astype(BF16)
            nm_v[mat, :, cols(my_cols + g * GRP, GRP)] = value.astype(BF16)

    def push(zh_, x_, mat, device, rows=None):
        s = cols((zh_ * 8 + x_ * 2 + c) * BLK, BLK)
        block = nm_v.at[:, :, s] if mat is None else nm_v.at[mat, :, s] if rows is None else nm_v.at[mat, rows, s]
        return send(block, block, device)

    sibs = []

    def share(zh_, x_, mat, rows=None):
        sibs.append(push(zh_, x_, mat, sibling, rows))

    def x_from(offset):
        return x_of(4 - offset)

    x_next = {1: x_peer[1], 3: x_peer[2]}
    part = {1: pl.ds(0, K // 2), 3: pl.ds(K // 2, K // 2)}
    z1c[3].wait_recv()
    for k in range(3):
        z2c[k].wait_recv()
    serve(1, [z1.at[3], z2.at[0], z2.at[1], z2.at[2]])
    gx1 = {o: push(zh, x, 1, x_next[o]) for o in (1, 3)}
    gz1 = push(zh, x, 1, partner)
    share(zh, x, 1)
    for copy in x1o:
        copy.wait_recv()
    x2c.wait_recv()
    serve(0, [x1.at[0, 1], x1.at[1, 1], x1.at[2, 1], x2])
    gz0 = push(zh, x, 0, partner)
    gx0 = {o: push(zh, x, 0, x_next[o]) for o in (1, 3)}
    share(zh, x, 0)
    hz, far = {}, {}
    for o in (1, 3):
        gx1[o].wait_recv()
        far[1, o] = push(zh, x_from(o), 1, x_next[o], part[o])
        hz[o] = push(zh, x_from(o), 1, partner)
        share(zh, x_from(o), 1)
    gz0.wait_recv()
    hx = {o: push(other, x, 0, x_next[o]) for o in (1, 3)}
    share(other, x, 0)
    gz1.wait_recv()
    share(other, x, 1)
    for o in (1, 3):
        gx0[o].wait_recv()
        far[0, o] = push(zh, x_from(o), 0, x_next[o], part[o])
        share(zh, x_from(o), 0)
    for o in (1, 3):
        far[1, o].wait_recv()
        hz[2, o] = push(zh, x_from(2), 1, partner, part[o])
        share(zh, x_from(2), 1, part[o])
    for o in (1, 3):
        hx[o].wait_recv()
        far[2, o] = push(other, x_from(o), 0, x_next[o], part[o])
        share(other, x_from(o), 0)
    for o in (1, 3):
        hz[o].wait_recv()
        share(other, x_from(o), 1)
        far[0, o].wait_recv()
        share(zh, x_from(2), 0, part[o])
    for o in (1, 3):
        hz[2, o].wait_recv()
        share(other, x_from(2), 1, part[o])
    for o in (1, 3):
        far[2, o].wait_recv()
        share(other, x_from(2), 0, part[o])
    for copy in sibs:
        copy.wait_recv()

    finish()


def store_kernel(a, b, c, d, a_out, b_out, c_out, d_out, sem):
    copies = [
        pltpu.make_async_copy(source, target, sem.at[i])
        for i, (source, target) in enumerate(((a, a_out), (b, b_out), (c, c_out), (d, d_out)))
    ]
    for copy in copies:
        copy.start()
    for copy in copies:
        copy.wait()


def body(*arrays):
    dma = pltpu.SemaphoreType.DMA
    vmem = pltpu.VMEM
    shapes = ((TOK, D), (2, K, D), (2, K, D), (2, K, BLK))
    results = pl.pallas_call(
        kernel,
        name="cascade",
        out_shape=tuple(pltpu.VMEM(shape, BF16) for shape in shapes),
        in_specs=[pl.BlockSpec(memory_space=pl.ANY)] * 8,
        out_specs=(pl.BlockSpec(memory_space=pltpu.VMEM),) * 4,
        scratch_shapes=[
            vmem((2, 2, TOK, D), BF16),
            vmem((K, D), BF16),
            vmem((K, D), BF16),
            vmem((K, D), BF16),
            vmem((2, K, D), BF16),
            vmem((2, K, D), BF16),
            vmem((2, K, BLK), BF16),
            vmem((4, 2, 2, 2, K, BLK), BF16),
            vmem((4, 2, 2, K, BLK), BF16),
            vmem((4, 2, 2, K, BLK), BF16),
            vmem((3, 2, K, BLK), BF16),
            vmem((K, BLK), BF16),
            vmem((4, K, BLK), BF16),
            vmem((3, K, BLK), BF16),
            vmem((K, 2 * TOK), F32),
            vmem((2, K, 2 * TOK), BF16),
            vmem((K, TOK), BF16),
            vmem((K, TOK), BF16),
            vmem((TOK, K), F32),
            vmem((K, TWO), F32),
            vmem((K, TWO), F32),
            dma((4,)), dma((4,)), dma((4,)), dma((4,)), dma((4,)), dma((80,)), dma((80,)),
        ],
        compiler_params=pltpu.CompilerParams(
            collective_id=0, has_side_effects=True, vmem_limit_bytes=44 * 2**20
        ),
        cost_estimate=pl.CostEstimate(flops=2_500_000_000, bytes_accessed=37_000_000, transcendentals=20_000),
    )(*arrays)
    stored = pl.pallas_call(
        store_kernel,
        name="store",
        out_shape=tuple(jax.ShapeDtypeStruct(shape, BF16) for shape in shapes),
        in_specs=[pl.BlockSpec(memory_space=pltpu.VMEM)] * 4,
        out_specs=(pl.BlockSpec(memory_space=pl.ANY),) * 4,
        scratch_shapes=[dma((4,))],
        compiler_params=pltpu.CompilerParams(vmem_limit_bytes=2 * 2**20),
        cost_estimate=pl.CostEstimate(flops=0, bytes_accessed=11_000_000, transcendentals=0),
    )(*results)
    return stored[0][None], stored[1][None], stored[2][None, None], stored[3][None]


def solution(mesh):
    return jax.shard_map(
        body,
        mesh=mesh,
        in_specs=(
            P("pipe", None, "rep", None),
            P("pipe", "rep", None),
            P("rep", None),
            P("pipe", None, None),
            P("pipe", None, None),
            P("pipe", None, None, None),
            P("pipe", "rep", None, None, None),
            P("pipe", None, None, "rep"),
        ),
        out_specs=(
            P("pipe", "rep", None),
            P("pipe", None, None, None),
            P("pipe", "rep", None, None, None),
            P("pipe", None, None, "rep"),
        ),
        check_vma=False,
    )
```
